128 devices in a mesh: prompt: 8 (over x, y_hi), resp: 16 (over z, y_lo, core).
Axes of the slice: x: 4, y: 4 (y_hi: 2, y_lo: 2; y = y_hi * 2 + y_lo), z: 4, core: 2. Of those that a mesh axis runs over, the one named last changes fastest.
Arguments:
- queries: bfloat16 [8, 16, 128, 8192], P('prompt', 'resp'), may hold values from -100 to 100
- response_key_rows: bfloat16 [8, 16, 128, 1024], P('prompt', 'resp'), may hold values from -5 to 5
- response_value_rows: bfloat16 [8, 16, 128, 1024], P('prompt', 'resp'), may hold values from -5 to 5
- prompt_keys: bfloat16 [8, 1024, 1024], P('prompt', 'resp'), may hold values from -6 to 6
- prompt_value_rows: bfloat16 [8, 1024, 1024], P('prompt', 'resp'), may hold values from -5 to 5
- out_grad: bfloat16 [8, 16, 128, 8192], P('prompt', 'resp'), may hold values from -5 to 5
- resp_lengths: int32 [8, 16], P('prompt', 'resp'), may hold values from 1 to 128, as said below
Outputs:
- attended: bfloat16 [8, 16, 128, 8192], P('prompt', 'resp')
- query_grad: bfloat16 [8, 16, 128, 8192], P('prompt', 'resp')
- resp_key_grad: bfloat16 [8, 16, 128, 1024], P('prompt', 'resp')
- resp_value_grad: bfloat16 [8, 16, 128, 1024], P('prompt', 'resp')
- prompt_key_grad: bfloat16 [8, 1024, 1024], P('prompt', 'resp')
- prompt_value_grad: bfloat16 [8, 1024, 1024], P('prompt', 'resp')
The draws below stay inside these ranges and needn't reach their ends.
Inputs may be any that keep to these rules, and one draw needn't show every extreme that they name: `resp_lengths`: one response in every draw has all 128 tokens live.
All inputs are finite; a program needn't handle non-finite values.
Results may differ from the reference program's by a relative error of at most 0.015.
Values may be sent and summed in bfloat16 or wider, within the bound.
A program may use at most 128 MiB of HBM per device.

```python
import jax
import jax.numpy as jnp
from jax import lax

QUERY_HEADS = 64
KEY_VALUE_HEADS = 8
HEAD_DIM = 128
RESPONSE_TOKENS = 128
PROMPT_COUNT = 8
RESPONSE_COUNT = 16
PROMPT_TOKENS = 1024


def draw_queries(key, part):
    key = jax.random.fold_in(key, 2)
    array_shape = (PROMPT_COUNT, RESPONSE_COUNT, RESPONSE_TOKENS, QUERY_HEADS * HEAD_DIM)
    return jnp.clip(jax.random.normal(key, array_shape, jnp.float32), -5.0, 5.0).astype(jnp.bfloat16)


def draw_prompt_keys(key, part):
    key = jax.random.fold_in(key, 1)
    array_shape = (PROMPT_COUNT, PROMPT_TOKENS, KEY_VALUE_HEADS * HEAD_DIM)
    return jnp.clip(jax.random.normal(key, array_shape, jnp.float32), -5.0, 5.0).astype(jnp.bfloat16)


def draw_resp_lengths(key, part):
    key = jax.random.fold_in(key, 5)
    count = PROMPT_COUNT * RESPONSE_COUNT
    index = jnp.arange(count, dtype=jnp.int32)
    ceiling = RESPONSE_TOKENS * (count - 1 + 2 * index) // (3 * (count - 1))
    floor_len = (ceiling + 1) // 2
    lengths = jax.random.randint(key, (count,), floor_len, ceiling + 1, jnp.int32)
    lengths = jnp.where(index == count - 1, RESPONSE_TOKENS, lengths)
    return lengths.reshape(PROMPT_COUNT, RESPONSE_COUNT)


def level_of(key, shape, cuts, least, high):
    def one(position, shards_of):
        steps = jax.random.uniform(jax.random.fold_in(jax.random.fold_in(key, 6), position), (shards_of,), jnp.float32, least / len(cuts), high / len(cuts))
        return jnp.repeat(jnp.exp(steps), shape[position] // shards_of).reshape((-1,) + (1,) * (len(shape) - position - 1))

    loudness = one(*cuts[0])
    for cut in cuts[1:]:
        loudness = loudness * one(*cut)
    return loudness


def scatter_about(stream_key, dims, scale, reach, pieces=(), held_as=jnp.bfloat16):
    drawn = scale * jax.random.normal(stream_key, dims, jnp.float32)
    if pieces:
        drawn = drawn * level_of(stream_key, dims, pieces, -0.22, 0.18)
    return jnp.clip(drawn, -reach, reach).astype(held_as)


def setup_inputs(seed: int = 0) -> dict:
    key_of = jax.random.split(jax.random.key(seed), 8)
    queries = draw_queries(jax.random.fold_in(key_of[7], 71), 0)
    response_key_rows = scatter_about(key_of[1], (PROMPT_COUNT, RESPONSE_COUNT, RESPONSE_TOKENS, KEY_VALUE_HEADS * HEAD_DIM), 1.0, 5.0, ((0, 8), (1, 16)))
    response_value_rows = scatter_about(key_of[2], (PROMPT_COUNT, RESPONSE_COUNT, RESPONSE_TOKENS, KEY_VALUE_HEADS * HEAD_DIM), 1.0, 5.0, ((0, 8), (1, 16)))
    prompt_keys = draw_prompt_keys(jax.random.fold_in(key_of[7], 71), 0)
    prompt_value_rows = scatter_about(key_of[4], (PROMPT_COUNT, PROMPT_TOKENS, KEY_VALUE_HEADS * HEAD_DIM), 1.0, 5.0, ((0, 8), (1, 16)))
    out_grad = scatter_about(key_of[5], (PROMPT_COUNT, RESPONSE_COUNT, RESPONSE_TOKENS, QUERY_HEADS * HEAD_DIM), 1.0, 5.0, ((0, 8), (1, 16)))
    resp_lengths = draw_resp_lengths(jax.random.fold_in(key_of[7], 71), 0)
    return dict(queries=queries, response_key_rows=response_key_rows, response_value_rows=response_value_rows, prompt_keys=prompt_keys, prompt_value_rows=prompt_value_rows, out_grad=out_grad, resp_lengths=resp_lengths)


def response_pass(queries, response_key_block, response_value_block, prompt_key_rows, prompt_value_block, grads, live, factor):
    row_count = queries.shape[0]
    plen = prompt_key_rows.shape[0]
    key_total_count = plen + row_count
    group_index = QUERY_HEADS // KEY_VALUE_HEADS
    inv = 1.0 / (HEAD_DIM ** 0.5)
    key_rows = jnp.concatenate([prompt_key_rows, response_key_block], 0).reshape(key_total_count, KEY_VALUE_HEADS, HEAD_DIM).transpose(1, 0, 2)
    value_rows = jnp.concatenate([prompt_value_block, response_value_block], 0).reshape(key_total_count, KEY_VALUE_HEADS, HEAD_DIM).transpose(1, 0, 2)
    live_rows = jnp.arange(row_count, dtype=jnp.int32) < live
    weight = jnp.where(live_rows, factor, jnp.float32(0.0))
    scaled_scores = (grads.astype(jnp.float32) * weight[:, None]).astype(jnp.bfloat16)
    query_rows = queries.reshape(row_count, KEY_VALUE_HEADS, group_index, HEAD_DIM).transpose(1, 2, 0, 3)
    group_size = scaled_scores.reshape(row_count, KEY_VALUE_HEADS, group_index, HEAD_DIM).transpose(1, 2, 0, 3)
    col = jnp.arange(key_total_count, dtype=jnp.int32)[None, :]
    row = jnp.arange(row_count, dtype=jnp.int32)[:, None]
    allowed = (col < plen) | (col - plen <= row)

    def one(parts):
        qg, gg, kg, vg = parts
        qf = qg.astype(jnp.float32)
        gf = gg.astype(jnp.float32)
        kf = kg.astype(jnp.float32)
        vf = vg.astype(jnp.float32)
        s = jnp.einsum('grd,kd->grk', qf, kf) * inv
        s = jnp.where(allowed[None], s, -jnp.inf)
        top = jnp.max(s, -1, keepdims=True)
        e = jnp.exp(s - top)
        p = e / jnp.sum(e, -1, keepdims=True)
        pb = p.astype(jnp.bfloat16)
        o = jnp.einsum('grk,kd->grd', pb.astype(jnp.float32), vf)
        delta = jnp.sum(gf * o, -1, keepdims=True)
        dp = jnp.einsum('grd,kd->grk', gf, vf)
        ds = (p * (dp - delta) * inv).astype(jnp.bfloat16)
        dsf = ds.astype(jnp.float32)
        dq = jnp.einsum('grk,kd->grd', dsf, kf).astype(jnp.bfloat16)
        dk = jnp.einsum('grk,grd->kd', dsf, qf)
        dv = jnp.einsum('grk,grd->kd', pb.astype(jnp.float32), gf)
        return o.astype(jnp.bfloat16), dq, dk, dv

    outs, dqs, key_gradients, value_gradients = lax.map(one, (query_rows, group_size, key_rows, value_rows))
    attended = outs.transpose(2, 0, 1, 3).reshape(row_count, QUERY_HEADS * HEAD_DIM)
    query_grad = dqs.transpose(2, 0, 1, 3).reshape(row_count, QUERY_HEADS * HEAD_DIM)
    gradient_keys = key_gradients.transpose(1, 0, 2).reshape(key_total_count, KEY_VALUE_HEADS * HEAD_DIM)
    gradient_values = value_gradients.transpose(1, 0, 2).reshape(key_total_count, KEY_VALUE_HEADS * HEAD_DIM)
    return (attended, query_grad, gradient_keys[plen:].astype(jnp.bfloat16), gradient_values[plen:].astype(jnp.bfloat16),
            gradient_keys[:plen], gradient_values[:plen])


def reference(queries, response_key_rows, response_value_rows, prompt_keys, prompt_value_rows, out_grad, resp_lengths):
    total = jnp.sum(resp_lengths.astype(jnp.float32))
    factor = jnp.float32(PROMPT_COUNT * RESPONSE_COUNT * RESPONSE_TOKENS) / total

    def per_prompt(args):
        q_g, kr_g, vr_g, kp_g, vp_g, d_g, len_g = args

        def per_resp(inner):
            q_r, kr_r, vr_r, d_r, len_r = inner
            return response_pass(q_r, kr_r, vr_r, kp_g, vp_g, d_r, len_r, factor)

        att, dq, dkr, dvr, dkp, dvp = lax.map(per_resp, (q_g, kr_g, vr_g, d_g, len_g))
        return att, dq, dkr, dvr, jnp.sum(dkp, 0).astype(jnp.bfloat16), jnp.sum(dvp, 0).astype(jnp.bfloat16)

    att, dq, dkr, dvr, dkp, dvp = lax.map(per_prompt, (queries, response_key_rows, response_value_rows, prompt_keys,
                                                       prompt_value_rows, out_grad, resp_lengths))
    return (att, dq, dkr, dvr, dkp, dvp)
```

```python
import jax
import jax.numpy as jnp
from jax import lax
from jax.experimental import pallas as pl
from jax.experimental.pallas import tpu as pltpu
from jax.sharding import PartitionSpec as P

F32, BF16 = jnp.float32, jnp.bfloat16
QUERY_HEADS = 64
KEY_VALUE_HEADS = 8
GROUP = QUERY_HEADS // KEY_VALUE_HEADS
D = 128
INV = 1.0 / D**0.5
LOG2E = 1.4426950408889634


def dot(a, b, ca, cb):
    return lax.dot_general(a, b, (((ca,), (cb,)), ((), ())), preferred_element_type=F32)


def attention_kernel(
    weight_ref, live_ref, q_ref, g_ref, kp_ref, vp_ref, kr_ref, vr_ref,
    att_ref, dq_ref, dkr_ref, dvr_ref, dkv_ref,
):
    tokens = q_ref.shape[0]
    heads = 4
    rows = heads * tokens
    plen = kp_ref.shape[0]
    factor = weight_ref[0, 0]
    live = live_ref[0, 0]
    token = lax.broadcasted_iota(jnp.int32, (rows, 128), 0) % tokens
    key = lax.broadcasted_iota(jnp.int32, (rows, 128), 1)
    seen = key <= token
    weight = jnp.where(token[:, :1] < live, factor, 0.0)

    def head(h, _):
        cols = pl.ds(pl.multiple_of(h * D, D), D)
        keys = jnp.concatenate([kp_ref[:, cols], kr_ref[:, cols]], 0)
        values = jnp.concatenate([vp_ref[:, cols], vr_ref[:, cols]], 0)

        def columns(j):
            return [
                pl.ds(pl.multiple_of((h * GROUP + j * heads + i) * D, D), D)
                for i in range(heads)
            ]

        def first(j):
            q = jnp.concatenate([q_ref[:, c] for c in columns(j)], 0)
            g = jnp.concatenate([g_ref[:, c] for c in columns(j)], 0)
            g = (g.astype(F32) * weight).astype(BF16)
            return q, g, dot(q, keys, 1, 1), dot(g, values, 1, 1)

        totals = [None, None]

        def rest(j, state):
            q, g, s, dp = state
            s = jnp.concatenate([s[:, :plen], jnp.where(seen, s[:, plen:], -1e30)], 1)
            top = jnp.max(s, 1, keepdims=True)
            e = jnp.exp2(s * (INV * LOG2E) - top * (INV * LOG2E))
            scale = 1.0 / jnp.sum(e, 1, keepdims=True)
            e = e.astype(BF16)
            o = dot(e, values, 1, 0) * scale
            gf = g.astype(F32)
            delta = jnp.sum(gf * o, 1, keepdims=True)
            ds = e * (dp - delta).astype(BF16)
            dq = dot(ds, keys, 1, 0) * (scale * INV)
            for i, c in enumerate(columns(j)):
                att_ref[:, c] = o[i * tokens : (i + 1) * tokens].astype(BF16)
                dq_ref[:, c] = dq[i * tokens : (i + 1) * tokens].astype(BF16)
            g = (gf * scale).astype(BF16)
            q = (q.astype(F32) * scale).astype(BF16)
            dk, dv = dot(q.T, ds, 1, 0), dot(g.T, e, 1, 0)
            totals[0] = dk if totals[0] is None else totals[0] + dk
            totals[1] = dv if totals[1] is None else totals[1] + dv

        state = first(0)
        for j in range(GROUP // heads):
            after = first(j + 1) if j + 1 < GROUP // heads else None
            rest(j, state)
            state = after
        dk = (totals[0].T * INV).astype(BF16)
        dv = totals[1].T.astype(BF16)
        dkr_ref[:, cols] = dk[plen:]
        dvr_ref[:, cols] = dv[plen:]
        dkv_ref[h, 0] = dk[:plen]
        dkv_ref[h, 1] = dv[:plen]
        return 0

    lax.fori_loop(0, KEY_VALUE_HEADS, head, 0)


def attention(weight, live, q, g, kp, vp, kr, vr):
    vmem = pl.BlockSpec(memory_space=pltpu.VMEM)
    smem = pl.BlockSpec(memory_space=pltpu.SMEM)
    return pl.pallas_call(
        attention_kernel,
        out_shape=(
            jax.ShapeDtypeStruct(q.shape, BF16),
            jax.ShapeDtypeStruct(q.shape, BF16),
            jax.ShapeDtypeStruct(kr.shape, BF16),
            jax.ShapeDtypeStruct(kr.shape, BF16),
            jax.ShapeDtypeStruct((KEY_VALUE_HEADS, 2, kp.shape[0], D), BF16),
        ),
        in_specs=[smem, smem] + [vmem] * 6,
        out_specs=(vmem,) * 5,
        compiler_params=pltpu.CompilerParams(vmem_limit_bytes=56 * 2**20),
        name="attention",
    )(weight, live, q, g, kp, vp, kr, vr)


def shards(q, kr, vr, kp, vp, g, lengths):
    rows, width = kp.shape[1:]
    kv = lax.all_gather(jnp.concatenate([kp, vp], 2), "resp", axis=1, tiled=True)[0]
    total = lax.psum(jnp.sum(lengths.astype(F32)), ("prompt", "resp"))
    slots = lax.axis_size("prompt") * lax.axis_size("resp") * q.shape[2]
    factor = jnp.full((1, 1), slots, F32) / total
    att, dq, dkr, dvr, dkv = attention(
        factor, lengths, q[0, 0], g[0, 0], kv[:, :width], kv[:, width:], kr[0, 0], vr[0, 0]
    )
    mine = lax.psum_scatter(dkv, "resp", scatter_dimension=2, tiled=True)
    mine = mine.transpose(1, 2, 0, 3).reshape(2, rows, width)
    return att[None, None], dq[None, None], dkr[None, None], dvr[None, None], mine[:1], mine[1:]


def solution(mesh):
    four = P("prompt", "resp", None, None)
    three = P("prompt", "resp", None)
    return jax.shard_map(
        shards,
        mesh=mesh,
        in_specs=(four, four, four, three, three, four, P("prompt", "resp")),
        out_specs=(four, four, four, four, three, three),
        check_vma=False,
    )
```

```python
import functools

import jax
import jax.numpy as jnp
from jax import lax
from jax.experimental import pallas as pl
from jax.experimental.pallas import tpu as pltpu
from jax.sharding import PartitionSpec as P

F32, BF16 = jnp.float32, jnp.bfloat16
QUERY_HEADS = 64
KEY_VALUE_HEADS = 8
GROUP = QUERY_HEADS // KEY_VALUE_HEADS
D = 128
INV = 1.0 / D**0.5
LOG2E = 1.4426950408889634
BLOCK_HEADS = 4
Z, Y, CORES = 4, 2, 2
MESH = pl.DeviceIdType.MESH


def dot(a, b, ca, cb):
    return lax.dot_general(a, b, (((ca,), (cb,)), ((), ())), preferred_element_type=F32)


def kernel(
    prompts, live_ref, q_hbm, g_hbm, kp_hbm, vp_hbm, kr_hbm, vr_hbm,
    att_hbm, dq_hbm, dkr_ref, dvr_ref, pk_ref, pv_ref,
    kv, q_ref, g_ref, att_ref, dq_ref, grad,
    pair_out, pair_in, far_out, far_in, near_out, near_in, last_out, last_in,
    lens_out, lens_in, factor_ref,
    load_sem, store_sem, ag_send, ag_recv, rs_send, rs_recv, len_send, len_recv,
):
    heads = KEY_VALUE_HEADS
    tokens = q_ref.shape[0]
    page = kp_hbm.shape[0]
    strip = Y * page
    plane = Z * strip
    plen = CORES * plane
    me = lax.axis_index("resp")
    prompt = lax.axis_index("prompt")
    z, y, c = me // (Y * CORES), (me // CORES) % Y, me % CORES
    up, down, over = (z + 1) % Z, (z + Z - 1) % Z, (z + 2) % Z

    def at(zz, yy, cc):
        return {"resp": (zz * Y + yy) * CORES + cc}

    sibling, beside = at(z, y, 1 - c), at(z, 1 - y, c)
    above, below = at(up, y, c), at(down, y, c)
    corner = at(z, 1 - y, 1 - c)
    len_peers = [
        [sibling, beside, corner],
        [above, below, at(over, y, c)],
        [{"prompt": (prompt + k) % prompts} for k in range(1, prompts)],
    ]

    def page_rows(cc, zz, yy):
        return pl.ds(pl.multiple_of(cc * plane + zz * strip + yy * page, page), page)

    def strip_rows(cc, zz):
        return pl.ds(pl.multiple_of(cc * plane + zz * strip, strip), strip)

    def plane_rows(cc):
        return pl.ds(pl.multiple_of(cc * plane, plane), plane)

    def columns(h):
        return pl.ds(pl.multiple_of(h * D, D), D)

    def block(h):
        return pl.ds(pl.multiple_of(h * GROUP * D, GROUP * D), GROUP * D)

    def load(h, i):
        mine, extra = page_rows(c, z, y), pl.ds(plen, tokens)
        src, dst = [
            lambda: (kp_hbm.at[:, columns(h)], kv.at[h, 0, mine, :]),
            lambda: (vp_hbm.at[:, columns(h)], kv.at[h, 1, mine, :]),
            lambda: (kr_hbm.at[:, columns(h)], kv.at[h, 0, extra, :]),
            lambda: (vr_hbm.at[:, columns(h)], kv.at[h, 1, extra, :]),
            lambda: (q_hbm.at[:, block(h)], q_ref.at[:, block(h)]),
            lambda: (g_hbm.at[:, block(h)], g_ref.at[:, block(h)]),
        ][i]()
        return pltpu.make_async_copy(src, dst, load_sem.at[h, i])

    def stores(h):
        return [
            pltpu.make_async_copy(a.at[:, block(h)], b.at[:, block(h)], store_sem.at[h, i])
            for i, (a, b) in enumerate([(att_ref, att_hbm), (dq_ref, dq_hbm)])
        ]

    def gather_copy(h, k, rows, to):
        return pltpu.make_async_remote_copy(
            kv.at[h, :, rows, :], kv.at[h, :, rows, :],
            ag_send.at[h, k], ag_recv.at[h, k], device_id=to, device_id_type=MESH,
        )

    def gather1(h):
        mine = page_rows(c, z, y)
        for i in range(2):
            load(h, i).wait()
        gather_copy(h, 0, mine, beside).start()
        gather_copy(h, 1, mine, above).start()
        gather_copy(h, 2, mine, below).start()
        gather_copy(h, 3, mine, sibling).start()

    def gather2(h):
        other = page_rows(c, z, 1 - y)
        gather_copy(h, 0, other, beside).wait_recv()
        gather_copy(h, 4, other, above).start()
        gather_copy(h, 5, other, below).start()
        gather_copy(h, 6, other, sibling).start()

    def gather3(h):
        gather_copy(h, 1, page_rows(c, down, y), below).wait_recv()
        gather_copy(h, 4, page_rows(c, down, 1 - y), below).wait_recv()
        gather_copy(h, 7, page_rows(c, down, 0), above).start()
        gather_copy(h, 2, page_rows(c, up, y), above).wait_recv()
        gather_copy(h, 5, page_rows(c, up, 1 - y), above).wait_recv()
        gather_copy(h, 8, page_rows(c, up, 1), below).start()
        gather_copy(h, 9, strip_rows(c, down), sibling).start()
        gather_copy(h, 10, strip_rows(c, up), sibling).start()

    def gather4(h):
        gather_copy(h, 7, page_rows(c, over, 0), below).wait_recv()
        gather_copy(h, 8, page_rows(c, over, 1), above).wait_recv()
        gather_copy(h, 11, strip_rows(c, over), sibling).start()

    def gathered(h):
        d = 1 - c
        gather_copy(h, 3, page_rows(d, z, y), sibling).wait_recv()
        gather_copy(h, 6, page_rows(d, z, 1 - y), sibling).wait_recv()
        gather_copy(h, 9, strip_rows(d, down), sibling).wait_recv()
        gather_copy(h, 10, strip_rows(d, up), sibling).wait_recv()
        gather_copy(h, 11, strip_rows(d, over), sibling).wait_recv()
        for i in range(2, 6):
            load(h, i).wait()

    def sum_ends(h, k):
        return [
            lambda: (pair_out.at[h], pair_in.at[h], sibling),
            lambda: (far_out.at[h, 0], far_in.at[h, 0], above),
            lambda: (far_out.at[h, 1], far_in.at[h, 1], below),
            lambda: (near_out.at[h, 0], near_in.at[h, 0], above),
            lambda: (near_out.at[h, 1], near_in.at[h, 1], below),
            lambda: (last_out.at[h], last_in.at[h], beside),
        ][k]()

    def sum_copy(h, k):
        src, dst, to = sum_ends(h, k)
        return pltpu.make_async_remote_copy(
            src, dst, rs_send.at[h, k], rs_recv.at[h, k], device_id=to, device_id_type=MESH
        )

    def sum0(h):
        pair_out[h] = grad[h % 4, :, plane_rows(1 - c), :].astype(BF16)
        sum_copy(h, 0).start()

    def sum1(h):
        sum_copy(h, 0).wait_recv()
        rows = plane_rows(c)
        grad[h % 4, :, rows, :] += pair_in[h].astype(F32)
        far_out[h, 0] = grad[h % 4, :, page_rows(c, over, 0), :].astype(BF16)
        sum_copy(h, 1).start()
        far_out[h, 1] = grad[h % 4, :, page_rows(c, over, 1), :].astype(BF16)
        sum_copy(h, 2).start()

    def sum2(h):
        sum_copy(h, 1).wait_recv()
        grad[h % 4, :, page_rows(c, up, 0), :] += far_in[h, 0].astype(F32)
        near_out[h, 0] = grad[h % 4, :, strip_rows(c, up), :].astype(BF16)
        sum_copy(h, 3).start()
        sum_copy(h, 2).wait_recv()
        grad[h % 4, :, page_rows(c, down, 1), :] += far_in[h, 1].astype(F32)
        near_out[h, 1] = grad[h % 4, :, strip_rows(c, down), :].astype(BF16)
        sum_copy(h, 4).start()

    def sum3(h):
        sum_copy(h, 3).wait_recv()
        sum_copy(h, 4).wait_recv()
        grad[h % 4, :, strip_rows(c, z), :] += near_in[h, 0].astype(F32) + near_in[h, 1].astype(F32)
        last_out[h] = grad[h % 4, :, page_rows(c, z, 1 - y), :].astype(BF16)
        sum_copy(h, 5).start()

    def sum4(h):
        sum_copy(h, 5).wait_recv()
        total = grad[h % 4, :, page_rows(c, z, y), :] + last_in[h].astype(F32)
        factor = factor_ref[0:1, :]
        pk_ref[:, columns(h)] = (total[0] * (factor * INV)).astype(BF16)
        pv_ref[:, columns(h)] = (total[1] * factor).astype(BF16)

    def len_slot(stage, i):
        return sum(len(p) for p in len_peers[:stage]) + i

    def len_copies(stage):
        return [
            pltpu.make_async_remote_copy(
                lens_out.at[stage], lens_in.at[len_slot(stage, i)],
                len_send.at[len_slot(stage, i)], len_recv.at[len_slot(stage, i)],
                device_id=peer, device_id_type=MESH,
            )
            for i, peer in enumerate(len_peers[stage])
        ]

    def len_start(stage):
        for copy in len_copies(stage):
            copy.start()

    def len_sum(stage):
        total = lens_out[stage]
        for i, copy in enumerate(len_copies(stage)):
            copy.wait_recv()
            total = total + lens_in[len_slot(stage, i)]
        return total

    rows = BLOCK_HEADS * tokens
    live = live_ref[0, 0]

    def first(h, j, keys, values):
        cols = [columns(h * GROUP + j * BLOCK_HEADS + i) for i in range(BLOCK_HEADS)]
        token = lax.broadcasted_iota(jnp.int32, (rows, 1), 0) % tokens
        q = jnp.concatenate([q_ref[:, k] for k in cols], 0)
        g = jnp.concatenate([g_ref[:, k] for k in cols], 0)
        g = jnp.where(token < live, g.astype(F32), 0.0).astype(BF16)
        return q, g, dot(q, keys, 1, 1), dot(g, values, 1, 1)

    def rest(h, j, keys, values, state, totals):
        q, g, s, dp = state
        cols = [columns(h * GROUP + j * BLOCK_HEADS + i) for i in range(BLOCK_HEADS)]
        token = lax.broadcasted_iota(jnp.int32, (rows, tokens), 0) % tokens
        key = lax.broadcasted_iota(jnp.int32, (rows, tokens), 1)
        s = jnp.concatenate([s[:, :plen], jnp.where(key <= token, s[:, plen:], -1e30)], 1)
        top = jnp.max(s, 1, keepdims=True)
        e = jnp.exp2(s * (INV * LOG2E) - top * (INV * LOG2E))
        scale = 1.0 / jnp.sum(e, 1, keepdims=True)
        e = e.astype(BF16)
        o = dot(e, values, 1, 0) * scale
        gf = g.astype(F32)
        delta = jnp.sum(gf * o, 1, keepdims=True)
        ds = e * (dp - delta).astype(BF16)
        dq = dot(ds, keys, 1, 0) * (scale * INV) * factor_ref[0:1, :]
        for i, k in enumerate(cols):
            att_ref[:, k] = o[i * tokens : (i + 1) * tokens].astype(BF16)
            dq_ref[:, k] = dq[i * tokens : (i + 1) * tokens].astype(BF16)
        g = (gf * scale).astype(BF16)
        q = (q.astype(F32) * scale).astype(BF16)
        dk, dv = dot(q.T, ds, 1, 0), dot(g.T, e, 1, 0)
        return (dk, dv) if totals is None else (totals[0] + dk, totals[1] + dv)

    def when(condition, stage, h):
        pl.when(condition)(functools.partial(stage, h))

    def head(h, _):
        when(h + 2 < heads, gather2, h + 2)
        when(h >= 2, sum2, h - 2)
        when(h >= 3, sum4, h - 3)
        gathered(h)
        keys, values = kv[h, 0], kv[h, 1]
        blocks = GROUP // BLOCK_HEADS
        state, totals = first(h, 0, keys, values), None
        for j in range(blocks):
            after = first(h, j + 1, keys, values) if j + 1 < blocks else None
            totals = rest(h, j, keys, values, state, totals)
            state = after
            if j == 0:
                when(h + 3 < heads, gather1, h + 3)
                when(h + 1 < heads, gather4, h + 1)
                when(h + 2 < heads, gather3, h + 2)
                when(h >= 1, sum1, h - 1)
                when(h >= 2, sum3, h - 2)
        dk, dv = totals[0].T, totals[1].T
        grad[h % 4, 0] = dk
        grad[h % 4, 1] = dv
        sum0(h)
        for copy in stores(h):
            copy.start()
        factor = factor_ref[0:1, :]
        dkr_ref[:, columns(h)] = (dk[plen:] * (factor * INV)).astype(BF16)
        dvr_ref[:, columns(h)] = (dv[plen:] * factor).astype(BF16)
        return 0

    def start_loads(h, _):
        for i in range(6):
            load(h, i).start()
        return 0

    lax.fori_loop(0, heads, start_loads, 0)
    lens_out[0] = jnp.full(lens_out.shape[1:], live.astype(F32))
    barrier = pltpu.get_barrier_semaphore()
    peers = [p for stage in len_peers for p in stage]
    for p in peers:
        pl.semaphore_signal(barrier, inc=1, device_id=p, device_id_type=MESH)
    pl.semaphore_wait(barrier, len(peers))

    gather1(0)
    len_start(0)
    gather1(1)
    gather2(0)
    lens_out[1] = len_sum(0)
    len_start(1)
    gather2(1)
    gather3(0)
    lens_out[2] = len_sum(1)
    len_start(2)
    gather1(2)
    gather4(0)
    gather3(1)
    factor_ref[...] = (prompts * Z * Y * CORES * tokens) / len_sum(2)

    lax.fori_loop(0, heads, head, 0)

    n = heads
    sum2(n - 2)
    sum4(n - 3)
    sum1(n - 1)
    sum3(n - 2)
    sum2(n - 1)
    sum4(n - 2)
    sum3(n - 1)
    sum4(n - 1)

    def finish(h, _):
        for k in range(12):
            rows_k = strip_rows(c, z) if k >= 9 else page_rows(c, z, y)
            gather_copy(h, k, rows_k, sibling).wait_send()
        for k in range(6):
            sum_copy(h, k).wait_send()
        for copy in stores(h):
            copy.wait()
        return 0

    lax.fori_loop(0, heads, finish, 0)
    for stage in range(3):
        for copy in len_copies(stage):
            copy.wait_send()


def attention(prompts, live, q, g, kp, vp, kr, vr):
    vmem = pl.BlockSpec(memory_space=pltpu.VMEM)
    smem = pl.BlockSpec(memory_space=pltpu.SMEM)
    anywhere = pl.BlockSpec(memory_space=pl.ANY)
    heads, tokens, page = KEY_VALUE_HEADS, q.shape[0], kp.shape[0]
    plane = Z * Y * page
    total = CORES * plane + tokens
    lens = 6 + prompts - 1
    dma = pltpu.SemaphoreType.DMA
    return pl.pallas_call(
        functools.partial(kernel, prompts),
        out_shape=(
            jax.ShapeDtypeStruct(q.shape, BF16),
            jax.ShapeDtypeStruct(q.shape, BF16),
            jax.ShapeDtypeStruct(kr.shape, BF16),
            jax.ShapeDtypeStruct(kr.shape, BF16),
            jax.ShapeDtypeStruct(kp.shape, BF16),
            jax.ShapeDtypeStruct(kp.shape, BF16),
        ),
        in_specs=[smem] + [anywhere] * 6,
        out_specs=(anywhere, anywhere, vmem, vmem, vmem, vmem),
        scratch_shapes=[
            pltpu.VMEM((heads, 2, total, D), BF16),
            pltpu.VMEM(q.shape, BF16),
            pltpu.VMEM(q.shape, BF16),
            pltpu.VMEM(q.shape, BF16),
            pltpu.VMEM(q.shape, BF16),
            pltpu.VMEM((4, 2, total, D), F32),
            pltpu.VMEM((heads, 2, plane, D), BF16),
            pltpu.VMEM((heads, 2, plane, D), BF16),
            pltpu.VMEM((heads, 2, 2, page, D), BF16),
            pltpu.VMEM((heads, 2, 2, page, D), BF16),
            pltpu.VMEM((heads, 2, 2, Y * page, D), BF16),
            pltpu.VMEM((heads, 2, 2, Y * page, D), BF16),
            pltpu.VMEM((heads, 2, page, D), BF16),
            pltpu.VMEM((heads, 2, page, D), BF16),
            pltpu.VMEM((3, 8, D), F32),
            pltpu.VMEM((lens, 8, D), F32),
            pltpu.VMEM((8, D), F32),
            dma((heads, 6)),
            dma((heads, 2)),
            dma((heads, 12)),
            dma((heads, 12)),
            dma((heads, 6)),
            dma((heads, 6)),
            dma((lens,)),
            dma((lens,)),
        ],
        compiler_params=pltpu.CompilerParams(
            collective_id=0, has_side_effects=True, vmem_limit_bytes=60 * 2**20
        ),
        name="attention",
    )(live, q, g, kp, vp, kr, vr)


def shards(q, kr, vr, kp, vp, g, lengths):
    att, dq, dkr, dvr, pk, pv = attention(
        lax.axis_size("prompt"), lengths, q[0, 0], g[0, 0], kp[0], vp[0], kr[0, 0], vr[0, 0]
    )
    return att[None, None], dq[None, None], dkr[None, None], dvr[None, None], pk[None], pv[None]


def solution(mesh):
    four = P("prompt", "resp", None, None)
    three = P("prompt", "resp", None)
    return jax.shard_map(
        shards,
        mesh=mesh,
        in_specs=(four, four, four, three, three, four, P("prompt", "resp")),
        out_specs=(four, four, four, four, three, three),
        check_vma=False,
    )
```

```python
import functools

import jax
import jax.numpy as jnp
from jax import lax
from jax.experimental import pallas as pl
from jax.experimental.pallas import tpu as pltpu
from jax.sharding import PartitionSpec as P

F32, BF16 = jnp.float32, jnp.bfloat16
QUERY_HEADS = 64
KEY_VALUE_HEADS = 8
GROUP = QUERY_HEADS // KEY_VALUE_HEADS
D = 128
INV = 1.0 / D**0.5
LOG2E = 1.4426950408889634
BLOCK_HEADS = 4
LAG = 4
Z, Y, CORES = 4, 2, 2
MESH = pl.DeviceIdType.MESH


def dot(a, b, ca, cb):
    return lax.dot_general(a, b, (((ca,), (cb,)), ((), ())), preferred_element_type=F32)


def kernel(
    prompts, live_ref, q_hbm, g_hbm, kp_hbm, vp_hbm, kr_hbm, vr_hbm,
    att_hbm, dq_hbm, dkr_ref, dvr_ref, pk_ref, pv_ref,
    kv, q_ref, g_ref, att_ref, dq_ref, grad,
    pair_out, pair_in, page_out, key_in, value_in, key_out2, key_in2, value_out2, value_in2, page_in, keep,
    ds_ref, scale_ref,
    lens_out, lens_in, factor_ref,
    load_sem, store_sem, ag_send, ag_recv, pair_send, pair_recv, rs_send, rs_recv,
    direct_send, direct_recv, len_send, len_recv,
):
    heads = KEY_VALUE_HEADS
    tokens = q_ref.shape[0]
    page = kp_hbm.shape[0]
    plane = Z * Y * page
    plen = CORES * plane
    me = lax.axis_index("resp")
    prompt = lax.axis_index("prompt")
    z, y, c = me // (Y * CORES), (me // CORES) % Y, me % CORES
    steps = (2, 1, 3)

    def place(zz, yy, cc):
        return {"resp": (zz * Y + yy) * CORES + cc}

    def ahead(i):
        return (z + steps[i]) % Z

    def behind(i):
        return (z + Z - steps[i]) % Z

    beside = place(z, 1 - y, c)
    sibling = place(z, y, 1 - c)
    len_peers = [
        [sibling],
        [beside],
        [place(ahead(i), y, c) for i in range(3)],
        [{"prompt": (prompt + k) % prompts} for k in range(2, prompts, 2)],
        [{"prompt": prompt + 1 - 2 * (prompt % 2)}],
    ]
    slots = [0, 1, 2, 5, 5 + prompts // 2 - 1]

    def page_rows(cc, zz, yy):
        return pl.ds(pl.multiple_of(cc * plane + (zz * Y + yy) * page, page), page)

    def plane_rows(cc):
        return pl.ds(pl.multiple_of(cc * plane, plane), plane)

    def columns(h):
        return pl.ds(pl.multiple_of(h * D, D), D)

    def block(h):
        return pl.ds(pl.multiple_of(h * GROUP * D, GROUP * D), GROUP * D)

    def load(h, i):
        mine, extra = page_rows(c, z, y), pl.ds(plen, tokens)
        src, dst = [
            lambda: (kp_hbm.at[:, columns(h)], kv.at[h, 0, mine, :]),
            lambda: (vp_hbm.at[:, columns(h)], kv.at[h, 1, mine, :]),
            lambda: (kr_hbm.at[:, columns(h)], kv.at[h, 0, extra, :]),
            lambda: (vr_hbm.at[:, columns(h)], kv.at[h, 1, extra, :]),
            lambda: (q_hbm.at[:, block(h)], q_ref.at[:, block(h)]),
            lambda: (g_hbm.at[:, block(h)], g_ref.at[:, block(h)]),
        ][i]()
        return pltpu.make_async_copy(src, dst, load_sem.at[h, i])

    def store(h, i):
        src, dst = [lambda: (att_ref, att_hbm), lambda: (dq_ref, dq_hbm)][i]()
        return pltpu.make_async_copy(src.at[:, block(h)], dst.at[:, block(h)], store_sem.at[h, i])

    def gather_copy(h, k, part, rows, to):
        piece = kv.at[h, part, rows, :]
        return pltpu.make_async_remote_copy(
            piece, piece, ag_send.at[h, k], ag_recv.at[h, k], device_id=to, device_id_type=MESH
        )

    both = slice(None)

    def gather_start(h):
        mine = page_rows(c, z, y)
        for i in range(2):
            load(h, i).wait()
        for i in range(3):
            gather_copy(h, i, both, mine, place(ahead(i), y, c)).start()
        gather_copy(h, 3, both, mine, beside).start()

    def gather_direct(h):
        mine = page_rows(c, z, y)
        for part in range(2):
            for i in range(3):
                gather_copy(h, 4 + 3 * part + i, part, mine, place(ahead(i), 1 - y, c)).start()

    def gather_wait(h):
        gather_copy(h, 3, both, page_rows(c, z, 1 - y), beside).wait_recv()
        for i in range(3):
            gather_copy(h, i, both, page_rows(c, behind(i), y), place(behind(i), y, c)).wait_recv()

    def gather_pass(h):
        gather_wait(h)
        for i in range(3):
            gather_copy(h, 4 + i, 0, page_rows(c, z, 1 - y), place(ahead(i), y, c)).start()
        for i in range(3):
            gather_copy(h, 7 + i, 1, page_rows(c, behind(i), y), beside).start()

    def gather_share(h):
        for part in range(2):
            for i in range(3):
                rows = page_rows(c, behind(i), 1 - y)
                gather_copy(h, 4 + 3 * part + i, part, rows, beside).wait_recv()
            gather_copy(h, 10 + part, part, plane_rows(c), sibling).start()

    def gathered(h):
        for part in range(2):
            gather_copy(h, 10 + part, part, plane_rows(1 - c), sibling).wait_recv()
        for i in range(2, 6):
            load(h, i).wait()

    def gather_sent(h):
        mine = page_rows(c, z, y)
        for k in range(12):
            part = both if k < 4 else (k - 4) // 3 if k < 10 else k - 10
            gather_copy(h, k, part, mine if k < 10 else plane_rows(c), sibling).wait_send()

    def pair_copy(h):
        return pltpu.make_async_remote_copy(
            pair_out.at[h], pair_in.at[h], pair_send.at[h], pair_recv.at[h],
            device_id=sibling, device_id_type=MESH,
        )

    def sum_copy(h, k):
        i = k if k < 3 else k - 5
        src, dst = [
            lambda: (page_out.at[h, 0, ahead(i)], key_in.at[h, i]),
            lambda: (page_out.at[h, 1, :, 1 - y], value_in.at[h]),
            lambda: (key_out2.at[h], key_in2.at[h]),
            lambda: (value_out2.at[h, ahead(i)], value_in2.at[h, i]),
        ][0 if k < 3 else k - 2 if k < 5 else 3]()
        to = beside if k in (3, 4) else place(ahead(i), y, c)
        return pltpu.make_async_remote_copy(
            src, dst, rs_send.at[h, k], rs_recv.at[h, k], device_id=to, device_id_type=MESH
        )

    def direct_copy(k):
        dz, dy = [(2, 1), (2, 0), (1, 1), (3, 1), (1, 0), (3, 0), (0, 1)][k]
        zz, yy = (z + dz) % Z, (y + dy) % Y
        return pltpu.make_async_remote_copy(
            page_out.at[heads - 1, :, zz, yy], page_in.at[k], direct_send.at[k], direct_recv.at[k],
            device_id=place(zz, yy, c), device_id_type=MESH,
        )

    def sum0(h):
        pair_out[h] = grad[h % 4, :, plane_rows(1 - c), :].astype(BF16)
        pair_copy(h).start()

    def sum_pair(h):
        pair_copy(h).wait_recv()
        total = grad[h % 4, :, plane_rows(c), :] + pair_in[h].astype(F32)
        page_out[h] = total.astype(BF16).reshape(page_out.shape[1:])

    def sum1(h):
        sum_pair(h)
        for k in range(4):
            sum_copy(h, k).start()

    def own(h, part, zz, yy):
        return grad[h % 4, part, page_rows(c, zz, yy), :] + pair_in[h, part, page_rows(0, zz, yy), :].astype(F32)

    def sum2(h):
        mine, other = own(h, 0, z, y), own(h, 0, z, 1 - y)
        for k in range(3):
            sum_copy(h, k).wait_recv()
            mine = mine + key_in[h, k, y].astype(F32)
            other = other + key_in[h, k, 1 - y].astype(F32)
        keep[h % 4, 0] = mine
        key_out2[h] = other.astype(BF16)
        sum_copy(h, 4).start()
        sum_copy(h, 3).wait_recv()
        for i in range(3):
            value_out2[h, ahead(i)] = (own(h, 1, ahead(i), y) + value_in[h, ahead(i)].astype(F32)).astype(BF16)
            sum_copy(h, 5 + i).start()
        keep[h % 4, 1] = own(h, 1, z, y) + value_in[h, z].astype(F32)

    def put(h, dk, dv):
        factor = factor_ref[0:1, :]
        pk_ref[:, columns(h)] = (dk * (factor * INV)).astype(BF16)
        pv_ref[:, columns(h)] = (dv * factor).astype(BF16)

    def sum3(h):
        sum_copy(h, 4).wait_recv()
        dk, dv = keep[h % 4, 0] + key_in2[h].astype(F32), keep[h % 4, 1]
        for i in range(3):
            sum_copy(h, 5 + i).wait_recv()
            dv = dv + value_in2[h, i].astype(F32)
        put(h, dk, dv)

    def direct1():
        sum_pair(heads - 1)
        for k in range(7):
            direct_copy(k).start()

    def direct2():
        dk, dv = own(heads - 1, 0, z, y), own(heads - 1, 1, z, y)
        for k in range(7):
            direct_copy(k).wait_recv()
            dk = dk + page_in[k, 0].astype(F32)
            dv = dv + page_in[k, 1].astype(F32)
        put(heads - 1, dk, dv)

    def len_slot(stage, i):
        return slots[stage] + i

    def len_copies(stage):
        return [
            pltpu.make_async_remote_copy(
                lens_out.at[stage], lens_in.at[len_slot(stage, i)],
                len_send.at[len_slot(stage, i)], len_recv.at[len_slot(stage, i)],
                device_id=peer, device_id_type=MESH,
            )
            for i, peer in enumerate(len_peers[stage])
        ]

    def len_start(stage):
        for copy in len_copies(stage):
            copy.start()

    def len_sum(stage):
        total = lens_out[stage]
        for i, copy in enumerate(len_copies(stage)):
            copy.wait_recv()
            total = total + lens_in[len_slot(stage, i)]
        return total

    def len_next(stage):
        lens_out[stage + 1] = len_sum(stage)
        len_start(stage + 1)

    def set_factor():
        factor_ref[...] = (prompts * Z * Y * CORES * tokens) / len_sum(4)

    rows = BLOCK_HEADS * tokens
    live = live_ref[0, 0]

    def first(h, j, keys, values):
        cols = [columns(h * GROUP + j * BLOCK_HEADS + i) for i in range(BLOCK_HEADS)]
        token = lax.broadcasted_iota(jnp.int32, (rows, 1), 0) % tokens
        q = jnp.concatenate([q_ref[:, k] for k in cols], 0)
        g = jnp.concatenate([g_ref[:, k] for k in cols], 0)
        g = jnp.where(token < live, g.astype(F32), 0.0).astype(BF16)
        return q, g, dot(q, keys, 1, 1), dot(g, values, 1, 1)

    def rest(h, j, values, state, totals):
        q, g, s, dp = state
        cols = [columns(h * GROUP + j * BLOCK_HEADS + i) for i in range(BLOCK_HEADS)]
        token = lax.broadcasted_iota(jnp.int32, (rows, tokens), 0) % tokens
        key = lax.broadcasted_iota(jnp.int32, (rows, tokens), 1)
        s = jnp.concatenate([s[:, :plen], jnp.where(key <= token, s[:, plen:], -1e30)], 1)
        top = jnp.max(s, 1, keepdims=True)
        e = jnp.exp2(s * (INV * LOG2E) - top * (INV * LOG2E))
        scale = 1.0 / jnp.sum(e, 1, keepdims=True)
        e = e.astype(BF16)
        o = dot(e, values, 1, 0) * scale
        for i, k in enumerate(cols):
            att_ref[:, k] = o[i * tokens : (i + 1) * tokens].astype(BF16)
        gf = g.astype(F32)
        delta = jnp.sum(gf * o, 1, keepdims=True)
        ds = e * (dp - delta).astype(BF16)
        g = (gf * scale).astype(BF16)
        q = (q.astype(F32) * scale).astype(BF16)
        dk, dv = dot(q.T, ds, 1, 0), dot(g.T, e, 1, 0)
        totals = (dk, dv) if totals is None else (totals[0] + dk, totals[1] + dv)
        place_rows = pl.ds(j * rows, rows)
        ds_ref[h % LAG, place_rows, :] = ds
        scale_ref[h % LAG, place_rows, :] = jnp.broadcast_to(scale * INV, (rows, D))
        return totals

    def query_grad(h, j, keys):
        cols = [columns(h * GROUP + j * BLOCK_HEADS + i) for i in range(BLOCK_HEADS)]
        place_rows = pl.ds(j * rows, rows)
        dq = dot(ds_ref[h % LAG, place_rows, :], keys, 1, 0)
        dq = dq * (scale_ref[h % LAG, place_rows, :] * factor_ref[0:1, :])
        for i, k in enumerate(cols):
            dq_ref[:, k] = dq[i * tokens : (i + 1) * tokens].astype(BF16)

    def resp_put(h):
        factor = factor_ref[0:1, :]
        dkr_ref[:, columns(h)] = (grad[h % 4, 0, plen:, :] * (factor * INV)).astype(BF16)
        dvr_ref[:, columns(h)] = (grad[h % 4, 1, plen:, :] * factor).astype(BF16)

    def when(condition, stage, h):
        pl.when(condition)(functools.partial(stage, h))

    def head(lagging, h, _):
        gathered(h)
        keys, values = kv[h, 0], kv[h, 1]
        blocks = GROUP // BLOCK_HEADS
        state, totals = first(h, 0, keys, values), None
        for j in range(blocks):
            after = first(h, j + 1, keys, values) if j + 1 < blocks else None
            if lagging:
                query_grad(h - LAG, j, kv[h - LAG, 0])
            totals = rest(h, j, values, state, totals)
            state = after
            if j == 0:
                for stage in range(1, 4):
                    pl.when(h == stage - 1)(functools.partial(len_next, stage))
                pl.when(h == 3)(set_factor)
                when(h + 3 < heads, gather_start, h + 3)
                when(h >= 1, sum1, h - 1)
                when(h + 2 < heads, gather_pass, h + 2)
                when(h + 1 < heads, gather_share, h + 1)
                when(h >= 2, sum2, h - 2)
                when(h >= 3, sum3, h - 3)
                when(h >= 3, resp_put, h - 3)
        grad[h % 4, 0] = totals[0].T
        grad[h % 4, 1] = totals[1].T
        sum0(h)
        store(h, 0).start()
        if lagging:
            store(h - LAG, 1).start()
        return 0

    def start_loads(h, _):
        for i in range(6):
            load(h, i).start()
        return 0

    lax.fori_loop(0, heads, start_loads, 0)
    lens_out[0] = jnp.full(lens_out.shape[1:], live.astype(F32))
    barrier = pltpu.get_barrier_semaphore()
    peers = [p for stage in len_peers for p in stage] + [place(ahead(i), 1 - y, c) for i in range(3)]
    for p in peers:
        pl.semaphore_signal(barrier, inc=1, device_id=p, device_id_type=MESH)
    pl.semaphore_wait(barrier, len(peers))

    for h in range(2):
        gather_start(h)
        gather_direct(h)
    len_start(0)
    gather_start(2)
    gather_wait(0)
    gather_share(0)
    len_next(0)
    gather_wait(1)

    lax.fori_loop(0, LAG, functools.partial(head, False), 0)
    lax.fori_loop(LAG, heads, functools.partial(head, True), 0)

    direct1()
    for h in range(heads - LAG, heads):
        keys = kv[h, 0]
        for j in range(GROUP // BLOCK_HEADS):
            query_grad(h, j, keys)
        store(h, 1).start()
        if h == heads - 2:
            sum2(heads - 2)
    for h in range(heads - 3, heads):
        resp_put(h)
    sum3(heads - 3)
    sum3(heads - 2)
    direct2()

    def finish(h, _):
        gather_sent(h)
        pair_copy(h).wait_send()
        for i in range(2):
            store(h, i).wait()
        return 0

    def summed(h, _):
        for k in range(8):
            sum_copy(h, k).wait_send()
        return 0

    lax.fori_loop(0, heads, finish, 0)
    lax.fori_loop(0, heads - 1, summed, 0)
    for k in range(7):
        direct_copy(k).wait_send()
    for stage in range(5):
        for copy in len_copies(stage):
            copy.wait_send()


def attention(prompts, live, q, g, kp, vp, kr, vr):
    vmem = pl.BlockSpec(memory_space=pltpu.VMEM)
    smem = pl.BlockSpec(memory_space=pltpu.SMEM)
    anywhere = pl.BlockSpec(memory_space=pl.ANY)
    heads, tokens, page = KEY_VALUE_HEADS, q.shape[0], kp.shape[0]
    plane = Z * Y * page
    total = CORES * plane + tokens
    lens = 6 + prompts // 2 - 1
    dma = pltpu.SemaphoreType.DMA
    return pl.pallas_call(
        functools.partial(kernel, prompts),
        out_shape=(
            jax.ShapeDtypeStruct(q.shape, BF16),
            jax.ShapeDtypeStruct(q.shape, BF16),
            jax.ShapeDtypeStruct(kr.shape, BF16),
            jax.ShapeDtypeStruct(kr.shape, BF16),
            jax.ShapeDtypeStruct(kp.shape, BF16),
            jax.ShapeDtypeStruct(kp.shape, BF16),
        ),
        in_specs=[smem] + [anywhere] * 6,
        out_specs=(anywhere, anywhere, vmem, vmem, vmem, vmem),
        scratch_shapes=[
            pltpu.VMEM((heads, 2, total, D), BF16),
            pltpu.VMEM(q.shape, BF16),
            pltpu.VMEM(q.shape, BF16),
            pltpu.VMEM(q.shape, BF16),
            pltpu.VMEM(q.shape, BF16),
            pltpu.VMEM((4, 2, total, D), F32),
            pltpu.VMEM((heads, 2, plane, D), BF16),
            pltpu.VMEM((heads, 2, plane, D), BF16),
            pltpu.VMEM((heads, 2, Z, Y, page, D), BF16),
            pltpu.VMEM((heads, 3, Y, page, D), BF16),
            pltpu.VMEM((heads, Z, page, D), BF16),
            pltpu.VMEM((heads, page, D), BF16),
            pltpu.VMEM((heads, page, D), BF16),
            pltpu.VMEM((heads, Z, page, D), BF16),
            pltpu.VMEM((heads, 3, page, D), BF16),
            pltpu.VMEM((7, 2, page, D), BF16),
            pltpu.VMEM((4, 2, page, D), F32),
            pltpu.VMEM((LAG, GROUP * tokens, total), BF16),
            pltpu.VMEM((LAG, GROUP * tokens, D), F32),
            pltpu.VMEM((5, 8, D), F32),
            pltpu.VMEM((lens, 8, D), F32),
            pltpu.VMEM((8, D), F32),
            dma((heads, 6)),
            dma((heads, 2)),
            dma((heads, 12)),
            dma((heads, 12)),
            dma((heads,)),
            dma((heads,)),
            dma((heads, 8)),
            dma((heads, 8)),
            dma((7,)),
            dma((7,)),
            dma((lens,)),
            dma((lens,)),
        ],
        compiler_params=pltpu.CompilerParams(
            collective_id=0, has_side_effects=True, vmem_limit_bytes=60 * 2**20
        ),
        name="attention",
    )(live, q, g, kp, vp, kr, vr)


def write_kernel(*refs):
    n = len(refs) // 3
    ins, outs, held = refs[:n], refs[n : 2 * n], refs[2 * n : 3 * n]
    read_sem, write_sem = refs[3 * n :]
    parts = []
    for a, b, v in zip(ins, outs, held):
        count = max(1, a.shape[1] // 2048)
        width = a.shape[1] // count
        parts += [(a, b, v, pl.ds(i * width, width)) for i in range(count)]

    def copies(i):
        a, b, v, cols = parts[i]
        return (
            pltpu.make_async_copy(a.at[:, cols], v.at[:, cols], read_sem.at[i]),
            pltpu.make_async_copy(v.at[:, cols], b.at[:, cols], write_sem.at[i]),
        )

    pairs = [copies(i) for i in range(len(parts))]
    for read, _ in pairs:
        read.start()
    for read, write in pairs:
        read.wait()
        write.start()
    for _, write in pairs:
        write.wait()


def write_out(*arrays):
    anywhere = pl.BlockSpec(memory_space=pl.ANY)
    return pl.pallas_call(
        write_kernel,
        out_shape=tuple(jax.ShapeDtypeStruct(a.shape, a.dtype) for a in arrays),
        in_specs=[anywhere] * len(arrays),
        out_specs=(anywhere,) * len(arrays),
        scratch_shapes=[pltpu.VMEM(a.shape, a.dtype) for a in arrays]
        + [pltpu.SemaphoreType.DMA((16,)), pltpu.SemaphoreType.DMA((16,))],
        compiler_params=pltpu.CompilerParams(vmem_limit_bytes=60 * 2**20),
        name="write_out",
    )(*arrays)


def shards(q, kr, vr, kp, vp, g, lengths):
    att, dq, dkr, dvr, pk, pv = attention(
        lax.axis_size("prompt"), lengths, q[0, 0], g[0, 0], kp[0], vp[0], kr[0, 0], vr[0, 0]
    )
    att, dq, dkr, dvr, pk, pv = write_out(att, dq, dkr, dvr, pk, pv)
    return att[None, None], dq[None, None], dkr[None, None], dvr[None, None], pk[None], pv[None]


def solution(mesh):
    four = P("prompt", "resp", None, None)
    three = P("prompt", "resp", None)
    return jax.shard_map(
        shards,
        mesh=mesh,
        in_specs=(four, four, four, three, three, four, P("prompt", "resp")),
        out_specs=(four, four, four, four, three, three),
        check_vma=False,
    )
```

```python
import functools

import jax
import jax.numpy as jnp
from jax import lax
from jax.experimental import pallas as pl
from jax.experimental.pallas import tpu as pltpu
from jax.sharding import PartitionSpec as P

F32, BF16 = jnp.float32, jnp.bfloat16
QUERY_HEADS = 64
KEY_VALUE_HEADS = 8
GROUP = QUERY_HEADS // KEY_VALUE_HEADS
D = 128
INV = 1.0 / D**0.5
LOG2E = 1.4426950408889634
BLOCK_HEADS = 4
LAG = 4
Z, Y, CORES = 4, 2, 2
MESH = pl.DeviceIdType.MESH


def dot(a, b, ca, cb):
    return lax.dot_general(a, b, (((ca,), (cb,)), ((), ())), preferred_element_type=F32)


def kernel(
    prompts, live_ref, q_hbm, g_hbm, kp_hbm, vp_hbm, kr_hbm, vr_hbm,
    att_ref, dq_ref, dkr_ref, dvr_ref, pk_ref, pv_ref,
    kv, q_ref, g_ref, grad,
    pair_out, pair_in, page_out, key_in, value_in, key_out2, key_in2, value_out2, value_in2, page_in, keep,
    ds_ref, scale_ref,
    lens_out, lens_in, factor_ref,
    load_sem, ag_send, ag_recv, pair_send, pair_recv, rs_send, rs_recv,
    direct_send, direct_recv, first_send, first_recv, len_send, len_recv,
):
    heads = KEY_VALUE_HEADS
    tokens = q_ref.shape[0]
    page = kp_hbm.shape[0]
    plane = Z * Y * page
    plen = CORES * plane
    me = lax.axis_index("resp")
    prompt = lax.axis_index("prompt")
    z, y, c = me // (Y * CORES), (me // CORES) % Y, me % CORES
    steps = (2, 1, 3)

    def place(zz, yy, cc):
        return {"resp": (zz * Y + yy) * CORES + cc}

    def ahead(i):
        return (z + steps[i]) % Z

    def behind(i):
        return (z + Z - steps[i]) % Z

    beside = place(z, 1 - y, c)
    sibling = place(z, y, 1 - c)
    len_peers = [
        [sibling],
        [beside],
        [place(ahead(i), y, c) for i in range(3)],
        [{"prompt": (prompt + k) % prompts} for k in range(2, prompts, 2)],
        [{"prompt": prompt + 1 - 2 * (prompt % 2)}],
    ]
    slots = [0, 1, 2, 5, 5 + prompts // 2 - 1]

    def page_rows(cc, zz, yy):
        return pl.ds(pl.multiple_of(cc * plane + (zz * Y + yy) * page, page), page)

    def plane_rows(cc):
        return pl.ds(pl.multiple_of(cc * plane, plane), plane)

    def columns(h):
        return pl.ds(pl.multiple_of(h * D, D), D)

    def block(h):
        return pl.ds(pl.multiple_of(h * GROUP * D, GROUP * D), GROUP * D)

    def load(h, i):
        mine, extra = page_rows(c, z, y), pl.ds(plen, tokens)
        src, dst = [
            lambda: (kp_hbm.at[:, columns(h)], kv.at[h, 0, mine, :]),
            lambda: (vp_hbm.at[:, columns(h)], kv.at[h, 1, mine, :]),
            lambda: (kr_hbm.at[:, columns(h)], kv.at[h, 0, extra, :]),
            lambda: (vr_hbm.at[:, columns(h)], kv.at[h, 1, extra, :]),
            lambda: (q_hbm.at[:, block(h)], q_ref.at[:, block(h)]),
            lambda: (g_hbm.at[:, block(h)], g_ref.at[:, block(h)]),
        ][i]()
        return pltpu.make_async_copy(src, dst, load_sem.at[h, i])

    def gather_copy(h, k, part, rows, to):
        piece = kv.at[h, part, rows, :]
        return pltpu.make_async_remote_copy(
            piece, piece, ag_send.at[h, k], ag_recv.at[h, k], device_id=to, device_id_type=MESH
        )

    both = slice(None)

    def gather_start(h):
        mine = page_rows(c, z, y)
        for i in range(2):
            load(h, i).wait()
        for i in range(3):
            gather_copy(h, i, both, mine, place(ahead(i), y, c)).start()
        gather_copy(h, 3, both, mine, beside).start()

    def gather_direct(h):
        mine = page_rows(c, z, y)
        for part in range(2):
            for i in range(3):
                gather_copy(h, 4 + 3 * part + i, part, mine, place(ahead(i), 1 - y, c)).start()

    def gather_wait(h):
        gather_copy(h, 3, both, page_rows(c, z, 1 - y), beside).wait_recv()
        for i in range(3):
            gather_copy(h, i, both, page_rows(c, behind(i), y), place(behind(i), y, c)).wait_recv()

    def gather_pass(h):
        gather_wait(h)
        for i in range(3):
            gather_copy(h, 4 + i, 0, page_rows(c, z, 1 - y), place(ahead(i), y, c)).start()
        for i in range(3):
            gather_copy(h, 7 + i, 1, page_rows(c, behind(i), y), beside).start()

    def gather_share(h):
        for part in range(2):
            for i in range(3):
                rows = page_rows(c, behind(i), 1 - y)
                gather_copy(h, 4 + 3 * part + i, part, rows, beside).wait_recv()
            gather_copy(h, 10 + part, part, plane_rows(c), sibling).start()

    def gathered_keys(h):
        gather_copy(h, 10, 0, plane_rows(1 - c), sibling).wait_recv()
        for i in (2, 4):
            load(h, i).wait()

    def gathered_values(h):
        gather_copy(h, 11, 1, plane_rows(1 - c), sibling).wait_recv()
        for i in (3, 5):
            load(h, i).wait()

    def first_copy(part, k, rows, to):
        if part == 0 or k > 3:
            return gather_copy(0, k, part, rows, to)
        piece = kv.at[0, 1, rows, :]
        return pltpu.make_async_remote_copy(
            piece, piece, first_send.at[k], first_recv.at[k], device_id=to, device_id_type=MESH
        )

    def first_start():
        mine = page_rows(c, z, y)
        for part in range(2):
            load(0, part).wait()
            for i in range(3):
                first_copy(part, i, mine, place(ahead(i), y, c)).start()
                first_copy(part, 4 + 3 * part + i, mine, place(ahead(i), 1 - y, c)).start()
            first_copy(part, 3, mine, beside).start()

    def first_share():
        for part in range(2):
            for i in range(3):
                first_copy(part, i, page_rows(c, behind(i), y), beside).wait_recv()
                first_copy(part, 4 + 3 * part + i, page_rows(c, behind(i), 1 - y), beside).wait_recv()
            first_copy(part, 3, page_rows(c, z, 1 - y), beside).wait_recv()
            gather_copy(0, 10 + part, part, plane_rows(c), sibling).start()

    def gather_sent(h, whole=slice(None)):
        mine = page_rows(c, z, y)
        for k in range(12):
            part = whole if k < 4 else (k - 4) // 3 if k < 10 else k - 10
            gather_copy(h, k, part, mine if k < 10 else plane_rows(c), sibling).wait_send()

    def pair_copy(h):
        return pltpu.make_async_remote_copy(
            pair_out.at[h], pair_in.at[h], pair_send.at[h], pair_recv.at[h],
            device_id=sibling, device_id_type=MESH,
        )

    def sum_copy(h, k):
        i = k if k < 3 else k - 5
        src, dst = [
            lambda: (page_out.at[h, 0, ahead(i)], key_in.at[h, i]),
            lambda: (page_out.at[h, 1, :, 1 - y], value_in.at[h]),
            lambda: (key_out2.at[h], key_in2.at[h]),
            lambda: (value_out2.at[h, ahead(i)], value_in2.at[h, i]),
        ][0 if k < 3 else k - 2 if k < 5 else 3]()
        to = beside if k in (3, 4) else place(ahead(i), y, c)
        return pltpu.make_async_remote_copy(
            src, dst, rs_send.at[h, k], rs_recv.at[h, k], device_id=to, device_id_type=MESH
        )

    def direct_copy(k):
        dz, dy = [(2, 1), (2, 0), (1, 1), (3, 1), (1, 0), (3, 0), (0, 1)][k]
        zz, yy = (z + dz) % Z, (y + dy) % Y
        return pltpu.make_async_remote_copy(
            page_out.at[heads - 1, :, zz, yy], page_in.at[k], direct_send.at[k], direct_recv.at[k],
            device_id=place(zz, yy, c), device_id_type=MESH,
        )

    def sum0(h):
        pair_out[h] = grad[h % 4, :, plane_rows(1 - c), :].astype(BF16)
        pair_copy(h).start()

    def sum_pair(h):
        pair_copy(h).wait_recv()
        total = grad[h % 4, :, plane_rows(c), :] + pair_in[h].astype(F32)
        page_out[h] = total.astype(BF16).reshape(page_out.shape[1:])

    def sum1(h):
        sum_pair(h)
        for k in range(4):
            sum_copy(h, k).start()

    def own(h, part, zz, yy):
        return grad[h % 4, part, page_rows(c, zz, yy), :] + pair_in[h, part, page_rows(0, zz, yy), :].astype(F32)

    def sum2(h):
        mine, other = own(h, 0, z, y), own(h, 0, z, 1 - y)
        for k in range(3):
            sum_copy(h, k).wait_recv()
            mine = mine + key_in[h, k, y].astype(F32)
            other = other + key_in[h, k, 1 - y].astype(F32)
        keep[h % 4, 0] = mine
        key_out2[h] = other.astype(BF16)
        sum_copy(h, 4).start()
        sum_copy(h, 3).wait_recv()
        for i in range(3):
            value_out2[h, ahead(i)] = (own(h, 1, ahead(i), y) + value_in[h, ahead(i)].astype(F32)).astype(BF16)
            sum_copy(h, 5 + i).start()
        keep[h % 4, 1] = own(h, 1, z, y) + value_in[h, z].astype(F32)

    def put(h, dk, dv):
        factor = factor_ref[0:1, :]
        pk_ref[:, columns(h)] = (dk * (factor * INV)).astype(BF16)
        pv_ref[:, columns(h)] = (dv * factor).astype(BF16)

    def sum3(h):
        sum_copy(h, 4).wait_recv()
        dk, dv = keep[h % 4, 0] + key_in2[h].astype(F32), keep[h % 4, 1]
        for i in range(3):
            sum_copy(h, 5 + i).wait_recv()
            dv = dv + value_in2[h, i].astype(F32)
        put(h, dk, dv)

    def direct1():
        sum_pair(heads - 1)
        for k in range(7):
            direct_copy(k).start()

    def direct2():
        dk, dv = own(heads - 1, 0, z, y), own(heads - 1, 1, z, y)
        for k in range(7):
            direct_copy(k).wait_recv()
            dk = dk + page_in[k, 0].astype(F32)
            dv = dv + page_in[k, 1].astype(F32)
        put(heads - 1, dk, dv)

    def len_slot(stage, i):
        return slots[stage] + i

    def len_copies(stage):
        return [
            pltpu.make_async_remote_copy(
                lens_out.at[stage], lens_in.at[len_slot(stage, i)],
                len_send.at[len_slot(stage, i)], len_recv.at[len_slot(stage, i)],
                device_id=peer, device_id_type=MESH,
            )
            for i, peer in enumerate(len_peers[stage])
        ]

    def len_start(stage):
        for copy in len_copies(stage):
            copy.start()

    def len_sum(stage):
        total = lens_out[stage]
        for i, copy in enumerate(len_copies(stage)):
            copy.wait_recv()
            total = total + lens_in[len_slot(stage, i)]
        return total

    def len_next(stage):
        lens_out[stage + 1] = len_sum(stage)
        len_start(stage + 1)

    def set_factor():
        factor_ref[...] = (prompts * Z * Y * CORES * tokens) / len_sum(4)

    rows = BLOCK_HEADS * tokens
    live = live_ref[0, 0]

    def first(h, j, keys):
        cols = [columns(h * GROUP + j * BLOCK_HEADS + i) for i in range(BLOCK_HEADS)]
        token = lax.broadcasted_iota(jnp.int32, (rows, 1), 0) % tokens
        q = jnp.concatenate([q_ref[:, k] for k in cols], 0)
        s = dot(q, keys, 1, 1)
        g = jnp.concatenate([g_ref[:, k] for k in cols], 0)
        g = jnp.where(token < live, g.astype(F32), 0.0).astype(BF16)
        return q, g, s, dot(g, kv[h, 1], 1, 1)

    def rest(h, j, values, state, totals):
        q, g, s, dp = state
        cols = [columns(h * GROUP + j * BLOCK_HEADS + i) for i in range(BLOCK_HEADS)]
        token = lax.broadcasted_iota(jnp.int32, (rows, tokens), 0) % tokens
        key = lax.broadcasted_iota(jnp.int32, (rows, tokens), 1)
        s = jnp.concatenate([s[:, :plen], jnp.where(key <= token, s[:, plen:], -1e30)], 1)
        top = jnp.max(s, 1, keepdims=True)
        e = jnp.exp2(s * (INV * LOG2E) - top * (INV * LOG2E))
        scale = 1.0 / jnp.sum(e, 1, keepdims=True)
        e = e.astype(BF16)
        o = dot(e, values, 1, 0) * scale
        for i, k in enumerate(cols):
            att_ref[:, k] = o[i * tokens : (i + 1) * tokens].astype(BF16)
        gf = g.astype(F32)
        delta = jnp.sum(gf * o, 1, keepdims=True)
        ds = e * (dp - delta).astype(BF16)
        g = (gf * scale).astype(BF16)
        q = (q.astype(F32) * scale).astype(BF16)
        dk, dv = dot(q.T, ds, 1, 0), dot(g.T, e, 1, 0)
        totals = (dk, dv) if totals is None else (totals[0] + dk, totals[1] + dv)
        place_rows = pl.ds(j * rows, rows)
        ds_ref[h % LAG, place_rows, :] = ds
        scale_ref[h % LAG, place_rows, :] = jnp.broadcast_to(scale * INV, (rows, D))
        return totals

    def query_grad(h, j, keys):
        cols = [columns(h * GROUP + j * BLOCK_HEADS + i) for i in range(BLOCK_HEADS)]
        place_rows = pl.ds(j * rows, rows)
        dq = dot(ds_ref[h % LAG, place_rows, :], keys, 1, 0)
        dq = dq * (scale_ref[h % LAG, place_rows, :] * factor_ref[0:1, :])
        for i, k in enumerate(cols):
            dq_ref[:, k] = dq[i * tokens : (i + 1) * tokens].astype(BF16)

    def resp_put(h):
        factor = factor_ref[0:1, :]
        dkr_ref[:, columns(h)] = (grad[h % 4, 0, plen:, :] * (factor * INV)).astype(BF16)
        dvr_ref[:, columns(h)] = (grad[h % 4, 1, plen:, :] * factor).astype(BF16)

    def when(condition, stage, h):
        pl.when(condition)(functools.partial(stage, h))

    def head(lagging, h, _):
        gathered_keys(h)
        gathered_values(h)
        for stage in range(1, 4):
            pl.when(h == stage - 1)(functools.partial(len_next, stage))
        pl.when(h == 3)(set_factor)
        when(h + 3 < heads, gather_start, h + 3)
        when(h >= 2, sum1, h - 2)
        when((h >= 1) & (h + 2 < heads), gather_pass, h + 2)
        when(h < 2, gather_wait, h + 1)
        when(h >= 3, sum2, h - 3)
        when(h >= 4, sum3, h - 4)
        when(h >= 4, resp_put, h - 4)
        when(h + 1 < heads, gather_share, h + 1)
        keys = kv[h, 0]
        blocks = GROUP // BLOCK_HEADS
        state, totals = first(h, 0, keys), None
        for j in range(blocks):
            after = first(h, j + 1, keys) if j + 1 < blocks else None
            if lagging:
                query_grad(h - LAG, j, kv[h - LAG, 0])
            totals = rest(h, j, kv[h, 1], state, totals)
            state = after
        grad[h % 4, 0] = totals[0].T
        grad[h % 4, 1] = totals[1].T
        sum0(h)
        return 0

    def start_loads(h, _):
        for i in range(6):
            load(h, i).start()
        return 0

    barrier = pltpu.get_barrier_semaphore()
    peers = [p for stage in len_peers for p in stage] + [place(ahead(i), 1 - y, c) for i in range(3)]
    for p in peers:
        pl.semaphore_signal(barrier, inc=1, device_id=p, device_id_type=MESH)
    lax.fori_loop(0, heads, start_loads, 0)
    lens_out[0] = jnp.full(lens_out.shape[1:], live.astype(F32))
    pl.semaphore_wait(barrier, len(peers))

    first_start()
    len_start(0)
    for h in range(1, 3):
        gather_start(h)
        gather_direct(h)
    first_share()
    len_next(0)

    lax.fori_loop(0, LAG, functools.partial(head, False), 0)
    lax.fori_loop(LAG, heads, functools.partial(head, True), 0)

    def last_query_grad(h):
        for j in range(GROUP // BLOCK_HEADS):
            query_grad(h, j, kv[h, 0])

    def finish(h, _):
        gather_sent(h)
        return 0

    def summed(h, _):
        pair_copy(h).wait_send()
        for k in range(8):
            sum_copy(h, k).wait_send()
        return 0

    n = heads
    sum1(n - 2)
    sum2(n - 3)
    last_query_grad(n - LAG)
    direct1()
    sum3(n - 4)
    for h in range(n - 4, n):
        resp_put(h)
    for h in range(n - LAG + 1, n - 1):
        last_query_grad(h)
    sum2(n - 2)
    sum3(n - 3)
    last_query_grad(n - 1)
    gather_sent(0, 0)
    for k in range(4):
        first_copy(1, k, page_rows(c, z, y), sibling).wait_send()
    lax.fori_loop(1, heads, finish, 0)
    lax.fori_loop(0, heads - 1, summed, 0)
    for stage in range(5):
        for copy in len_copies(stage):
            copy.wait_send()
    sum3(n - 2)
    direct2()
    pair_copy(n - 1).wait_send()
    for k in range(7):
        direct_copy(k).wait_send()


def attention(prompts, live, q, g, kp, vp, kr, vr):
    vmem = pl.BlockSpec(memory_space=pltpu.VMEM)
    smem = pl.BlockSpec(memory_space=pltpu.SMEM)
    anywhere = pl.BlockSpec(memory_space=pl.ANY)
    heads, tokens, page = KEY_VALUE_HEADS, q.shape[0], kp.shape[0]
    plane = Z * Y * page
    total = CORES * plane + tokens
    lens = 6 + prompts // 2 - 1
    dma = pltpu.SemaphoreType.DMA
    return pl.pallas_call(
        functools.partial(kernel, prompts),
        out_shape=tuple(pltpu.VMEM(a.shape, BF16) for a in (q, q, kr, kr, kp, kp)),
        in_specs=[smem] + [anywhere] * 6,
        out_specs=(vmem,) * 6,
        scratch_shapes=[
            pltpu.VMEM((heads, 2, total, D), BF16),
            pltpu.VMEM(q.shape, BF16),
            pltpu.VMEM(q.shape, BF16),
            pltpu.VMEM((4, 2, total, D), F32),
            pltpu.VMEM((heads, 2, plane, D), BF16),
            pltpu.VMEM((heads, 2, plane, D), BF16),
            pltpu.VMEM((heads, 2, Z, Y, page, D), BF16),
            pltpu.VMEM((heads, 3, Y, page, D), BF16),
            pltpu.VMEM((heads, Z, page, D), BF16),
            pltpu.VMEM((heads, page, D), BF16),
            pltpu.VMEM((heads, page, D), BF16),
            pltpu.VMEM((heads, Z, page, D), BF16),
            pltpu.VMEM((heads, 3, page, D), BF16),
            pltpu.VMEM((7, 2, page, D), BF16),
            pltpu.VMEM((4, 2, page, D), F32),
            pltpu.VMEM((LAG, GROUP * tokens, total), BF16),
            pltpu.VMEM((LAG, GROUP * tokens, D), F32),
            pltpu.VMEM((5, 8, D), F32),
            pltpu.VMEM((lens, 8, D), F32),
            pltpu.VMEM((8, D), F32),
            dma((heads, 6)),
            dma((heads, 12)),
            dma((heads, 12)),
            dma((heads,)),
            dma((heads,)),
            dma((heads, 8)),
            dma((heads, 8)),
            dma((7,)),
            dma((7,)),
            dma((4,)),
            dma((4,)),
            dma((lens,)),
            dma((lens,)),
        ],
        compiler_params=pltpu.CompilerParams(
            collective_id=0, has_side_effects=True, vmem_limit_bytes=59 * 2**20
        ),
        name="attention",
    )(live, q, g, kp, vp, kr, vr)


def shards(q, kr, vr, kp, vp, g, lengths):
    att, dq, dkr, dvr, pk, pv = attention(
        lax.axis_size("prompt"), lengths, q[0, 0], g[0, 0], kp[0], vp[0], kr[0, 0], vr[0, 0]
    )
    return att[None, None], dq[None, None], dkr[None, None], dvr[None, None], pk[None], pv[None]


def solution(mesh):
    four = P("prompt", "resp", None, None)
    three = P("prompt", "resp", None)
    return jax.shard_map(
        shards,
        mesh=mesh,
        in_specs=(four, four, four, three, three, four, P("prompt", "resp")),
        out_specs=(four, four, four, four, three, three),
        check_vma=False,
    )
```

```python
import functools

import jax
import jax.numpy as jnp
from jax import lax
from jax.experimental import pallas as pl
from jax.experimental.pallas import tpu as pltpu
from jax.sharding import PartitionSpec as P

F32, BF16 = jnp.float32, jnp.bfloat16
QUERY_HEADS = 64
KEY_VALUE_HEADS = 8
GROUP = QUERY_HEADS // KEY_VALUE_HEADS
D = 128
INV = 1.0 / D**0.5
LOG2E = 1.4426950408889634
BLOCK_HEADS = 4
LAG = 4
Z, Y, CORES = 4, 2, 2
MESH = pl.DeviceIdType.MESH


def dot(a, b, ca, cb):
    return lax.dot_general(a, b, (((ca,), (cb,)), ((), ())), preferred_element_type=F32)


def kernel(
    prompts, live_ref, q_hbm, g_hbm, kp_hbm, vp_hbm, kr_hbm, vr_hbm,
    att_ref, dq_ref, dkr_ref, dvr_ref, pk_ref, pv_ref,
    kv, q_ref, g_ref, grad,
    pair_out, pair_in, page_out, key_in, value_in, key_out2, key_in2, value_out2, value_in2, page_in, keep,
    ds_ref, scale_ref,
    lens_out, lens_in, factor_ref,
    load_sem, ag_send, ag_recv, pair_send, pair_recv, rs_send, rs_recv,
    direct_send, direct_recv, first_send, first_recv, len_send, len_recv,
):
    heads = KEY_VALUE_HEADS
    tokens = q_ref.shape[0]
    page = kp_hbm.shape[0]
    plane = Z * Y * page
    plen = CORES * plane
    me = lax.axis_index("resp")
    prompt = lax.axis_index("prompt")
    z, y, c = me // (Y * CORES), (me // CORES) % Y, me % CORES
    steps = (2, 1, 3)

    def place(zz, yy, cc):
        return {"resp": (zz * Y + yy) * CORES + cc}

    def ahead(i):
        return (z + steps[i]) % Z

    def behind(i):
        return (z + Z - steps[i]) % Z

    beside = place(z, 1 - y, c)
    sibling = place(z, y, 1 - c)
    len_peers = [
        [sibling],
        [beside],
        [place(ahead(i), y, c) for i in range(3)],
        [{"prompt": (prompt + k) % prompts} for k in range(2, prompts, 2)],
        [{"prompt": prompt + 1 - 2 * (prompt % 2)}],
    ]
    slots = [0, 1, 2, 5, 5 + prompts // 2 - 1]

    def page_rows(cc, zz, yy):
        return pl.ds(pl.multiple_of(cc * plane + (zz * Y + yy) * page, page), page)

    def plane_rows(cc):
        return pl.ds(pl.multiple_of(cc * plane, plane), plane)

    def columns(h):
        return pl.ds(pl.multiple_of(h * D, D), D)

    def block(h):
        return pl.ds(pl.multiple_of(h * GROUP * D, GROUP * D), GROUP * D)

    def load(h, i):
        mine, extra = page_rows(c, z, y), pl.ds(plen, tokens)
        src, dst = [
            lambda: (kp_hbm.at[:, columns(h)], kv.at[h, 0, mine, :]),
            lambda: (vp_hbm.at[:, columns(h)], kv.at[h, 1, mine, :]),
            lambda: (kr_hbm.at[:, columns(h)], kv.at[h, 0, extra, :]),
            lambda: (vr_hbm.at[:, columns(h)], kv.at[h, 1, extra, :]),
            lambda: (q_hbm.at[:, block(h)], q_ref.at[:, block(h)]),
            lambda: (g_hbm.at[:, block(h)], g_ref.at[:, block(h)]),
        ][i]()
        return pltpu.make_async_copy(src, dst, load_sem.at[h, i])

    def gather_copy(h, k, part, rows, to):
        piece = kv.at[h, part, rows, :]
        return pltpu.make_async_remote_copy(
            piece, piece, ag_send.at[h, k], ag_recv.at[h, k], device_id=to, device_id_type=MESH
        )

    both = slice(None)

    def gather_start(h):
        mine = page_rows(c, z, y)
        for i in range(2):
            load(h, i).wait()
        for i in range(3):
            gather_copy(h, i, both, mine, place(ahead(i), y, c)).start()
        gather_copy(h, 3, both, mine, beside).start()

    def gather_direct(h):
        mine = page_rows(c, z, y)
        for part in range(2):
            for i in range(3):
                gather_copy(h, 4 + 3 * part + i, part, mine, place(ahead(i), 1 - y, c)).start()

    def gather_wait(h):
        gather_copy(h, 3, both, page_rows(c, z, 1 - y), beside).wait_recv()
        for i in range(3):
            gather_copy(h, i, both, page_rows(c, behind(i), y), place(behind(i), y, c)).wait_recv()

    def gather_pass(h):
        gather_wait(h)
        for i in range(3):
            gather_copy(h, 4 + i, 0, page_rows(c, z, 1 - y), place(ahead(i), y, c)).start()
        for i in range(3):
            gather_copy(h, 7 + i, 1, page_rows(c, behind(i), y), beside).start()

    def gather_share(h):
        for part in range(2):
            for i in range(3):
                rows = page_rows(c, behind(i), 1 - y)
                gather_copy(h, 4 + 3 * part + i, part, rows, beside).wait_recv()
            gather_copy(h, 10 + part, part, plane_rows(c), sibling).start()

    def gathered_keys(h):
        gather_copy(h, 10, 0, plane_rows(1 - c), sibling).wait_recv()
        for i in (2, 4):
            load(h, i).wait()

    def gathered_values(h):
        gather_copy(h, 11, 1, plane_rows(1 - c), sibling).wait_recv()
        for i in (3, 5):
            load(h, i).wait()

    def first_copy(part, k, rows, to):
        if part == 0 or k > 3:
            return gather_copy(0, k, part, rows, to)
        piece = kv.at[0, 1, rows, :]
        return pltpu.make_async_remote_copy(
            piece, piece, first_send.at[k], first_recv.at[k], device_id=to, device_id_type=MESH
        )

    def first_start():
        mine = page_rows(c, z, y)
        for part in range(2):
            load(0, part).wait()
            for i in range(3):
                first_copy(part, i, mine, place(ahead(i), y, c)).start()
                first_copy(part, 4 + 3 * part + i, mine, place(ahead(i), 1 - y, c)).start()
            first_copy(part, 3, mine, beside).start()

    def first_share():
        for part in range(2):
            for i in range(3):
                first_copy(part, i, page_rows(c, behind(i), y), beside).wait_recv()
                first_copy(part, 4 + 3 * part + i, page_rows(c, behind(i), 1 - y), beside).wait_recv()
            first_copy(part, 3, page_rows(c, z, 1 - y), beside).wait_recv()
            gather_copy(0, 10 + part, part, plane_rows(c), sibling).start()

    def gather_sent(h, whole=slice(None)):
        mine = page_rows(c, z, y)
        for k in range(12):
            part = whole if k < 4 else (k - 4) // 3 if k < 10 else k - 10
            gather_copy(h, k, part, mine if k < 10 else plane_rows(c), sibling).wait_send()

    def pair_copy(h):
        return pltpu.make_async_remote_copy(
            pair_out.at[h], pair_in.at[h], pair_send.at[h], pair_recv.at[h],
            device_id=sibling, device_id_type=MESH,
        )

    def sum_copy(h, k):
        i = k if k < 3 else k - 5
        src, dst = [
            lambda: (page_out.at[h, 0, ahead(i)], key_in.at[h, i]),
            lambda: (page_out.at[h, 1, :, 1 - y], value_in.at[h]),
            lambda: (key_out2.at[h], key_in2.at[h]),
            lambda: (value_out2.at[h, ahead(i)], value_in2.at[h, i]),
        ][0 if k < 3 else k - 2 if k < 5 else 3]()
        to = beside if k in (3, 4) else place(ahead(i), y, c)
        return pltpu.make_async_remote_copy(
            src, dst, rs_send.at[h, k], rs_recv.at[h, k], device_id=to, device_id_type=MESH
        )

    def direct_copy(k):
        dz, dy = [(2, 1), (2, 0), (1, 1), (3, 1), (1, 0), (3, 0), (0, 1)][k]
        zz, yy = (z + dz) % Z, (y + dy) % Y
        return pltpu.make_async_remote_copy(
            page_out.at[heads - 1, :, zz, yy], page_in.at[k], direct_send.at[k], direct_recv.at[k],
            device_id=place(zz, yy, c), device_id_type=MESH,
        )

    def sum0(h):
        pair_out[h] = grad[h % 4, :, plane_rows(1 - c), :].astype(BF16)
        pair_copy(h).start()

    def sum_pair(h):
        pair_copy(h).wait_recv()
        total = grad[h % 4, :, plane_rows(c), :] + pair_in[h].astype(F32)
        page_out[h] = total.astype(BF16).reshape(page_out.shape[1:])

    def sum1(h):
        sum_pair(h)
        for k in range(4):
            sum_copy(h, k).start()

    def own(h, part, zz, yy):
        return grad[h % 4, part, page_rows(c, zz, yy), :] + pair_in[h, part, page_rows(0, zz, yy), :].astype(F32)

    def sum2(h):
        mine, other = own(h, 0, z, y), own(h, 0, z, 1 - y)
        for k in range(3):
            sum_copy(h, k).wait_recv()
            mine = mine + key_in[h, k, y].astype(F32)
            other = other + key_in[h, k, 1 - y].astype(F32)
        keep[h % 4, 0] = mine
        key_out2[h] = other.astype(BF16)
        sum_copy(h, 4).start()
        sum_copy(h, 3).wait_recv()
        for i in range(3):
            value_out2[h, ahead(i)] = (own(h, 1, ahead(i), y) + value_in[h, ahead(i)].astype(F32)).astype(BF16)
            sum_copy(h, 5 + i).start()
        keep[h % 4, 1] = own(h, 1, z, y) + value_in[h, z].astype(F32)

    def put(h, dk, dv):
        factor = factor_ref[0:1, :]
        pk_ref[:, columns(h)] = (dk * (factor * INV)).astype(BF16)
        pv_ref[:, columns(h)] = (dv * factor).astype(BF16)

    def sum3(h):
        sum_copy(h, 4).wait_recv()
        dk, dv = keep[h % 4, 0] + key_in2[h].astype(F32), keep[h % 4, 1]
        for i in range(3):
            sum_copy(h, 5 + i).wait_recv()
            dv = dv + value_in2[h, i].astype(F32)
        put(h, dk, dv)

    def direct1():
        sum_pair(heads - 1)
        for k in range(7):
            direct_copy(k).start()

    def direct2():
        dk, dv = own(heads - 1, 0, z, y), own(heads - 1, 1, z, y)
        for k in range(7):
            direct_copy(k).wait_recv()
            dk = dk + page_in[k, 0].astype(F32)
            dv = dv + page_in[k, 1].astype(F32)
        put(heads - 1, dk, dv)

    def len_slot(stage, i):
        return slots[stage] + i

    def len_copies(stage):
        return [
            pltpu.make_async_remote_copy(
                lens_out.at[stage], lens_in.at[len_slot(stage, i)],
                len_send.at[len_slot(stage, i)], len_recv.at[len_slot(stage, i)],
                device_id=peer, device_id_type=MESH,
            )
            for i, peer in enumerate(len_peers[stage])
        ]

    def len_start(stage):
        for copy in len_copies(stage):
            copy.start()

    def len_sum(stage):
        total = lens_out[stage]
        for i, copy in enumerate(len_copies(stage)):
            copy.wait_recv()
            total = total + lens_in[len_slot(stage, i)]
        return total

    def len_next(stage):
        lens_out[stage + 1] = len_sum(stage)
        len_start(stage + 1)

    def set_factor():
        factor_ref[...] = (prompts * Z * Y * CORES * tokens) / len_sum(4)

    rows = BLOCK_HEADS * tokens
    live = live_ref[0, 0]

    def first(h, j, keys):
        cols = [columns(h * GROUP + j * BLOCK_HEADS + i) for i in range(BLOCK_HEADS)]
        token = lax.broadcasted_iota(jnp.int32, (rows, 1), 0) % tokens
        q = jnp.concatenate([q_ref[:, k] for k in cols], 0)
        s = dot(q, keys, 1, 1)
        g = jnp.concatenate([g_ref[:, k] for k in cols], 0)
        g = jnp.where(token < live, g.astype(F32), 0.0).astype(BF16)
        return q, g, s, dot(g, kv[h, 1], 1, 1)

    def rest(h, j, values, state, totals):
        q, g, s, dp = state
        cols = [columns(h * GROUP + j * BLOCK_HEADS + i) for i in range(BLOCK_HEADS)]
        token = lax.broadcasted_iota(jnp.int32, (rows, tokens), 0) % tokens
        key = lax.broadcasted_iota(jnp.int32, (rows, tokens), 1)
        s = jnp.concatenate([s[:, :plen], jnp.where(key <= token, s[:, plen:], -1e30)], 1)
        top = jnp.max(s, 1, keepdims=True)
        e = jnp.exp2(s * (INV * LOG2E) - top * (INV * LOG2E))
        scale = 1.0 / jnp.sum(e, 1, keepdims=True)
        e = e.astype(BF16)
        o = dot(e, values, 1, 0) * scale
        for i, k in enumerate(cols):
            att_ref[:, k] = o[i * tokens : (i + 1) * tokens].astype(BF16)
        gf = g.astype(F32)
        delta = jnp.sum(gf * o, 1, keepdims=True)
        ds = e * (dp - delta).astype(BF16)
        g = (gf * scale).astype(BF16)
        q = (q.astype(F32) * scale).astype(BF16)
        dk, dv = dot(q.T, ds, 1, 0), dot(g.T, e, 1, 0)
        totals = (dk, dv) if totals is None else (totals[0] + dk, totals[1] + dv)
        place_rows = pl.ds(j * rows, rows)
        ds_ref[h % LAG, place_rows, :] = ds
        scale_ref[h % LAG, place_rows, :] = jnp.broadcast_to(scale * INV, (rows, D))
        return totals

    def query_grad(h, j, keys):
        cols = [columns(h * GROUP + j * BLOCK_HEADS + i) for i in range(BLOCK_HEADS)]
        place_rows = pl.ds(j * rows, rows)
        dq = dot(ds_ref[h % LAG, place_rows, :], keys, 1, 0)
        dq = dq * (scale_ref[h % LAG, place_rows, :] * factor_ref[0:1, :])
        for i, k in enumerate(cols):
            dq_ref[:, k] = dq[i * tokens : (i + 1) * tokens].astype(BF16)

    def resp_put(h):
        factor = factor_ref[0:1, :]
        dkr_ref[:, columns(h)] = (grad[h % 4, 0, plen:, :] * (factor * INV)).astype(BF16)
        dvr_ref[:, columns(h)] = (grad[h % 4, 1, plen:, :] * factor).astype(BF16)

    def when(condition, stage, h):
        pl.when(condition)(functools.partial(stage, h))

    def head(lagging, h, _):
        gathered_keys(h)
        gathered_values(h)
        for stage in range(1, 4):
            pl.when(h == stage - 1)(functools.partial(len_next, stage))
        pl.when(h == 3)(set_factor)
        when(h + 3 < heads, gather_start, h + 3)
        when(h >= 2, sum1, h - 2)
        when((h >= 1) & (h + 2 < heads), gather_pass, h + 2)
        when(h < 2, gather_wait, h + 1)
        when(h >= 3, sum2, h - 3)
        when(h >= 4, sum3, h - 4)
        when(h >= 4, resp_put, h - 4)
        when(h + 1 < heads, gather_share, h + 1)
        keys = kv[h, 0]
        blocks = GROUP // BLOCK_HEADS
        state, totals = first(h, 0, keys), None
        for j in range(blocks):
            after = first(h, j + 1, keys) if j + 1 < blocks else None
            if lagging:
                query_grad(h - LAG, j, kv[h - LAG, 0])
            totals = rest(h, j, kv[h, 1], state, totals)
            state = after
        grad[h % 4, 0] = totals[0].T
        grad[h % 4, 1] = totals[1].T
        sum0(h)
        return 0

    def start_loads(h, _):
        for i in range(6):
            load(h, i).start()
        return 0

    barrier = pltpu.get_barrier_semaphore()
    peers = [p for stage in len_peers for p in stage] + [place(ahead(i), 1 - y, c) for i in range(3)]
    for p in peers:
        pl.semaphore_signal(barrier, inc=1, device_id=p, device_id_type=MESH)
    lax.fori_loop(0, heads, start_loads, 0)
    lens_out[0] = jnp.full(lens_out.shape[1:], live.astype(F32))
    pl.semaphore_wait(barrier, len(peers))

    first_start()
    len_start(0)
    for h in range(1, 3):
        gather_start(h)
        gather_direct(h)
    first_share()
    len_next(0)

    lax.fori_loop(0, LAG, functools.partial(head, False), 0)
    lax.fori_loop(LAG, heads, functools.partial(head, True), 0)

    def last_query_grad(h):
        for j in range(GROUP // BLOCK_HEADS):
            query_grad(h, j, kv[h, 0])

    def finish(h, _):
        gather_sent(h)
        return 0

    def summed(h, _):
        pair_copy(h).wait_send()
        for k in range(8):
            sum_copy(h, k).wait_send()
        return 0

    n = heads
    sum1(n - 2)
    sum2(n - 3)
    last_query_grad(n - LAG)
    direct1()
    sum3(n - 4)
    for h in range(n - 4, n):
        resp_put(h)
    for h in range(n - LAG + 1, n - 1):
        last_query_grad(h)
    sum2(n - 2)
    sum3(n - 3)
    last_query_grad(n - 1)
    gather_sent(0, 0)
    for k in range(4):
        first_copy(1, k, page_rows(c, z, y), sibling).wait_send()
    lax.fori_loop(1, heads, finish, 0)
    lax.fori_loop(0, heads - 1, summed, 0)
    for stage in range(5):
        for copy in len_copies(stage):
            copy.wait_send()
    sum3(n - 2)
    direct2()
    pair_copy(n - 1).wait_send()
    for k in range(7):
        direct_copy(k).wait_send()


def attention(prompts, live, q, g, kp, vp, kr, vr):
    vmem = pl.BlockSpec(memory_space=pltpu.VMEM)
    smem = pl.BlockSpec(memory_space=pltpu.SMEM)
    anywhere = pl.BlockSpec(memory_space=pl.ANY)
    heads, tokens, page = KEY_VALUE_HEADS, q.shape[0], kp.shape[0]
    plane = Z * Y * page
    total = CORES * plane + tokens
    lens = 6 + prompts // 2 - 1
    dma = pltpu.SemaphoreType.DMA
    return pl.pallas_call(
        functools.partial(kernel, prompts),
        out_shape=tuple(pltpu.VMEM(a.shape, BF16) for a in (q, q, kr, kr, kp, kp)),
        in_specs=[smem] + [anywhere] * 6,
        out_specs=(vmem,) * 6,
        scratch_shapes=[
            pltpu.VMEM((heads, 2, total, D), BF16),
            pltpu.VMEM(q.shape, BF16),
            pltpu.VMEM(q.shape, BF16),
            pltpu.VMEM((4, 2, total, D), F32),
            pltpu.VMEM((heads, 2, plane, D), BF16),
            pltpu.VMEM((heads, 2, plane, D), BF16),
            pltpu.VMEM((heads, 2, Z, Y, page, D), BF16),
            pltpu.VMEM((heads, 3, Y, page, D), BF16),
            pltpu.VMEM((heads, Z, page, D), BF16),
            pltpu.VMEM((heads, page, D), BF16),
            pltpu.VMEM((heads, page, D), BF16),
            pltpu.VMEM((heads, Z, page, D), BF16),
            pltpu.VMEM((heads, 3, page, D), BF16),
            pltpu.VMEM((7, 2, page, D), BF16),
            pltpu.VMEM((4, 2, page, D), F32),
            pltpu.VMEM((LAG, GROUP * tokens, total), BF16),
            pltpu.VMEM((LAG, GROUP * tokens, D), F32),
            pltpu.VMEM((5, 8, D), F32),
            pltpu.VMEM((lens, 8, D), F32),
            pltpu.VMEM((8, D), F32),
            dma((heads, 6)),
            dma((heads, 12)),
            dma((heads, 12)),
            dma((heads,)),
            dma((heads,)),
            dma((heads, 8)),
            dma((heads, 8)),
            dma((7,)),
            dma((7,)),
            dma((4,)),
            dma((4,)),
            dma((lens,)),
            dma((lens,)),
        ],
        compiler_params=pltpu.CompilerParams(
            collective_id=0, has_side_effects=True, vmem_limit_bytes=59 * 2**20
        ),
        name="attention",
    )(live, q, g, kp, vp, kr, vr)


def write_kernel(*refs):
    n = len(refs) // 2
    copies = [
        pltpu.make_async_copy(a, b, refs[2 * n].at[i])
        for i, (a, b) in enumerate(zip(refs[:n], refs[n : 2 * n]))
    ]
    for copy in copies:
        copy.start()
    for copy in copies:
        copy.wait()


def write_out(*arrays):
    return pl.pallas_call(
        write_kernel,
        out_shape=tuple(pltpu.HBM(a.shape, a.dtype) for a in arrays),
        in_specs=[pl.BlockSpec(memory_space=pltpu.VMEM)] * len(arrays),
        out_specs=(pl.BlockSpec(memory_space=pltpu.HBM),) * len(arrays),
        scratch_shapes=[pltpu.SemaphoreType.DMA((len(arrays),))],
        compiler_params=pltpu.CompilerParams(vmem_limit_bytes=2 * 2**20),
        name="write_out",
    )(*arrays)


def shards(q, kr, vr, kp, vp, g, lengths):
    att, dq, dkr, dvr, pk, pv = attention(
        lax.axis_size("prompt"), lengths, q[0, 0], g[0, 0], kp[0], vp[0], kr[0, 0], vr[0, 0]
    )
    att, dq, dkr, dvr, pk, pv = write_out(att, dq, dkr, dvr, pk, pv)
    return att[None, None], dq[None, None], dkr[None, None], dvr[None, None], pk[None], pv[None]


def solution(mesh):
    four = P("prompt", "resp", None, None)
    three = P("prompt", "resp", None)
    return jax.shard_map(
        shards,
        mesh=mesh,
        in_specs=(four, four, four, three, three, four, P("prompt", "resp")),
        out_specs=(four, four, four, four, three, three),
        check_vma=False,
    )
```
